32 devices in a mesh: grp: 4 (over y, x), shard: 8 (over z, core).
Axes of the slice: x: 2, y: 2, z: 4, core: 2. Of those that a mesh axis runs over, the one named last changes fastest.
Arguments:
- moe_input: bfloat16 [4096, 2048], P(('grp', 'shard')), may hold values from -6 to 6
- out_grad: bfloat16 [4096, 2048], P(('grp', 'shard')), may hold values from -6 to 6
- expert_ids: int32 [4096, 2], P(('grp', 'shard')), may hold values from 0 to 127, all different within a row; in each aligned block of 128 rows (0 to 127, 128 to 255, ...) at most 3 rows name the same one
- gate_weights: bfloat16 [4096, 2], P(('grp', 'shard')), may hold values from 0.099609375 to 1
- w_gate: bfloat16 [128, 768, 2048], P('shard', 'grp'), may hold values from -0.125 to 0.125
- w_up: bfloat16 [128, 768, 2048], P('shard', 'grp'), may hold values from -0.125 to 0.125
- w_down: bfloat16 [128, 768, 2048], P('shard', 'grp'), may hold values from -0.21875 to 0.21875
Outputs:
- input_grad: bfloat16 [4096, 2048], P(('grp', 'shard'))
- grad_gate: bfloat16 [128, 768, 2048], P('shard', 'grp')
- grad_up: bfloat16 [128, 768, 2048], P('shard', 'grp')
- grad_down: bfloat16 [128, 768, 2048], P('shard', 'grp')
The draws below stay inside these ranges and needn't reach their ends.
Inputs may be any that keep to these rules, and one draw needn't show every extreme that they name: `expert_ids`: each token names 2 different experts; within the 128 tokens of one device no expert is named more than 3 times, a bound that some block reaches.
All inputs are finite; a program needn't handle non-finite values.
Results may differ from the reference program's by a relative error of at most 0.0058.
Values may be sent and summed in bfloat16 or wider, within the bound.
A program may use at most 192 MiB of HBM per device.

```python
import math
import jax
import jax.numpy as jnp
import numpy as np
from jax import lax

D = 2048
FF = 768
EXPERTS = 128
TOP = 2
TOK_DEV = 128
CAP = 3
TOKENS = 4096


def level_of(stream_key, extent, pieces, low, high):
    def one(dim, blocks):
        heights = jax.random.uniform(jax.random.fold_in(jax.random.fold_in(stream_key, 6), dim), (blocks,), jnp.float32, low / len(pieces), high / len(pieces))
        return jnp.repeat(jnp.exp(heights), extent[dim] // blocks).reshape((-1,) + (1,) * (len(extent) - dim - 1))

    gain = one(*pieces[0])
    for cut in pieces[1:]:
        gain = gain * one(*cut)
    return gain


def deal_out(own_key, own, number, rows, number_of, top, bound, lean):
    sequence = jax.random.permutation(own_key, number_of)
    packed, ordinary = shares(number_of, rows * top, bound, lean, True), shares(number_of, rows * top, bound, lean, False)
    places = jnp.arange(number_of)

    def named(sizes, rotation):
        used = int((sizes > 0).sum())
        fixed = max(1, used // 4)
        moved = fixed + (places - fixed + rotation * (used - fixed)) % max(1, number_of - fixed)
        return jnp.zeros((number_of,), jnp.int32).at[sequence[jnp.where(places < fixed, places, moved)]].set(jnp.asarray(sizes, jnp.int32))

    sizes = jnp.where(number % 4 == 0, named(packed, number // 4), named(ordinary, number - number // 4 - 1))
    mixed = jax.random.permutation(jax.random.fold_in(own, 3), number_of)
    source_of, receiver = mixed[0:number_of // 2 * 2:2], mixed[1:number_of // 2 * 2:2]
    slack = jnp.minimum(sizes[source_of] - 1, bound - sizes[receiver]) // 2
    slack = jnp.where((source_of == sequence[0]) | (receiver == sequence[0]) | (sizes[receiver] == 0), 0, jnp.maximum(slack, 0))
    moved = jax.random.randint(jax.random.fold_in(own, 4), (number_of // 2,), 0, 1 << 20) % (slack + 1)
    sizes = sizes.at[source_of].add(-moved).at[receiver].add(moved)
    items = jnp.searchsorted(jnp.cumsum(sizes), jnp.arange(rows * top), side="right").astype(jnp.int32)
    grid = items.reshape(top, rows).T
    grid = grid[jax.random.permutation(jax.random.fold_in(own, 1), rows)]
    rotation = jax.random.randint(jax.random.fold_in(own, 2), (rows, 1), 0, top)
    return jnp.take_along_axis(grid, (jnp.arange(top)[None, :] + rotation) % top, axis=1)


def shares(count, total, bound, skew, full):
    weights = [(1 << 20) // math.isqrt(rank ** skew) + 1 for rank in range(1, count + 1)]
    largest = bound if full else min(bound, max(-(-total // count), total * weights[0] // sum(weights)))
    least = 1 if total - largest >= count - 1 else 0
    counts, spare = [largest] + [least] * (count - 1), total - largest - least * (count - 1)
    while spare > 0:
        movable = [i for i in range(1, count) if counts[i] < largest] or [i for i in range(1, count) if counts[i] < bound]
        pool, budget = sum([weights[i] for i in movable]), spare
        for i in movable:
            addition = min(bound - counts[i], max(1, budget * weights[i] // pool), spare)
            counts[i] = counts[i] + addition
            spare = spare - addition
    return np.array(counts)


def centred(rng, dims, spread, reach, pieces=(), held_as=jnp.bfloat16):
    drawn = jax.random.normal(rng, dims, jnp.float32) * spread
    if len(pieces) > 0:
        drawn = level_of(rng, dims, pieces, -0.22, 0.18) * drawn
    return jnp.clip(drawn, min=-reach, max=reach).astype(held_as)


def setup_inputs(seed: int = 0) -> dict:
    arg_keys = jax.random.split(jax.random.key(seed), 8)
    moe_input = centred(arg_keys[0], (TOKENS, D), 1.0, 6.0, ((0, 32),))
    out_grad = centred(arg_keys[1], (TOKENS, D), 1.0, 6.0, ((0, 32),))
    expert_ids_keys = jax.random.split(jax.random.fold_in(arg_keys[2], 1), TOKENS // TOK_DEV)
    expert_ids_turns = jax.random.permutation(jax.random.fold_in(arg_keys[2], 3), TOKENS // TOK_DEV)
    expert_ids = jax.vmap(lambda own, number: deal_out(jax.random.fold_in(arg_keys[2], 2), own, number, TOK_DEV, EXPERTS, TOP, CAP, 1))(expert_ids_keys, expert_ids_turns).reshape((TOKENS, TOP))
    gate_weights = jnp.clip(0.099609375 + 0.9003906 * jax.random.uniform(arg_keys[3], (TOKENS, TOP), jnp.float32) ** level_of(arg_keys[3], (TOKENS, TOP), ((0, 32),), -0.2, 0.2), 0.099609375, 1.0).astype(jnp.bfloat16)
    w_gate = centred(arg_keys[4], (EXPERTS, FF, D), D ** -0.5, 0.125, ((0, 8), (1, 4)))
    w_up = centred(arg_keys[5], (EXPERTS, FF, D), D ** -0.5, 0.125, ((0, 8), (1, 4)))
    w_down = centred(arg_keys[6], (EXPERTS, FF, D), FF ** -0.5, 0.21875, ((0, 8), (1, 4)))
    return {"moe_input": moe_input, "out_grad": out_grad, "expert_ids": expert_ids, "gate_weights": gate_weights, "w_gate": w_gate, "w_up": w_up, "w_down": w_down}


def silu_parts(pre_act):
    sigmoid_val = jax.nn.sigmoid(pre_act)
    return pre_act * sigmoid_val, sigmoid_val * (1.0 + pre_act * (1.0 - sigmoid_val))


def reference(moe_input, out_grad, expert_ids, gate_weights, w_gate, w_up, w_down):
    contract = (((1,), (1,)), ((), ()))
    contract_rows = (((0,), (0,)), ((), ()))
    blocks = TOKENS // TOK_DEV
    flat_ids = expert_ids.reshape(blocks, TOK_DEV * TOP)
    matches = (flat_ids[:, :, None] == jnp.arange(EXPERTS, dtype=jnp.int32)[None, None, :]).astype(jnp.int32)
    rank_of = jnp.sum((jnp.cumsum(matches, axis=1) - matches) * matches, axis=2).astype(jnp.int32)
    block_of = jnp.broadcast_to(jnp.arange(blocks, dtype=jnp.int32)[:, None], flat_ids.shape)
    token_of = block_of * TOK_DEV + jnp.broadcast_to(jnp.arange(TOK_DEV * TOP, dtype=jnp.int32)[None, :] // TOP, flat_ids.shape)
    slot_table = jnp.zeros((EXPERTS, blocks, CAP), jnp.int32).at[flat_ids, block_of, rank_of].set(token_of + 1)
    gate_table = jnp.zeros((EXPERTS, blocks, CAP), jnp.float32).at[flat_ids, block_of, rank_of].set(
        gate_weights.reshape(blocks, TOK_DEV * TOP).astype(jnp.float32))

    def expert_step(running, expert_item):
        row_index, gate_vals, weight_gate, weight_up, weight_down = expert_item
        occupied = row_index > 0
        position = jnp.maximum(row_index - 1, 0).astype(jnp.int32)
        inputs = jnp.where(occupied[:, None], moe_input[position], jnp.zeros((), moe_input.dtype))
        grads_in = jnp.where(occupied[:, None], out_grad[position], jnp.zeros((), out_grad.dtype))
        gated = (gate_vals[:, None] * grads_in.astype(jnp.float32)).astype(jnp.bfloat16)
        pre_gate = lax.dot_general(inputs, weight_gate, contract, preferred_element_type=jnp.float32)
        pre_up = lax.dot_general(inputs, weight_up, contract, preferred_element_type=jnp.float32)
        act_val, act_slope = silu_parts(pre_gate)
        activation = (act_val * pre_up).astype(jnp.bfloat16)
        act_grad = lax.dot_general(gated, weight_down, contract, preferred_element_type=jnp.float32)
        gate_grad = (act_grad * pre_up * act_slope).astype(jnp.bfloat16)
        up_grad = (act_grad * act_val).astype(jnp.bfloat16)
        down_sum = lax.dot_general(activation, gated, contract_rows, preferred_element_type=jnp.float32)
        gate_sum = lax.dot_general(gate_grad, inputs, contract_rows, preferred_element_type=jnp.float32)
        up_sum = lax.dot_general(up_grad, inputs, contract_rows, preferred_element_type=jnp.float32)
        terms = jnp.dot(gate_grad, weight_gate, preferred_element_type=jnp.float32) + jnp.dot(up_grad, weight_up, preferred_element_type=jnp.float32)
        running = running.at[position].add(jnp.where(occupied[:, None], terms, jnp.zeros((), terms.dtype)))
        return running, (gate_sum.astype(jnp.bfloat16), up_sum.astype(jnp.bfloat16), down_sum.astype(jnp.bfloat16))

    moe_grad, grads = lax.scan(
        expert_step,
        jnp.zeros((TOKENS, D), jnp.float32),
        (slot_table.reshape(EXPERTS, blocks * CAP), gate_table.reshape(EXPERTS, blocks * CAP), w_gate, w_up, w_down))
    input_grad = (out_grad.astype(jnp.float32) + moe_grad).astype(jnp.bfloat16)
    return input_grad, grads[0], grads[1], grads[2]
```

```python
import functools

import jax
import jax.numpy as jnp
from jax import lax
from jax.experimental import pallas as pl
from jax.experimental.pallas import tpu as pltpu
from jax.sharding import PartitionSpec as P

EXPERTS = 128
TOP = 2
CAP = 3
TILE = 16
PER_TILE = TILE // CAP
MESH = pl.DeviceIdType.MESH
F32 = jnp.float32
BF16 = jnp.bfloat16


def silu_parts(pre_act):
    sigmoid_val = jax.nn.sigmoid(pre_act)
    return (pre_act * sigmoid_val, sigmoid_val * (1.0 + pre_act * (1.0 - sigmoid_val)))


def flip(index, bits):
    bit = 1
    while bit <= bits:
        if bits & bit:
            index = index + bit * (1 - 2 * ((index // bit) % 2))
        bit *= 2
    return index


def places(shards):
    grp, me = lax.axis_index("grp"), lax.axis_index("shard")
    peers = [flip(me, k) for k in range(shards)]
    return grp, me, flip(grp, 1), flip(grp, 2), flip(grp, 3), peers


def greet(grp, me, grp_x, grp_y, peers):
    barrier = pltpu.get_barrier_semaphore()
    for peer in peers[1:]:
        pl.semaphore_signal(barrier, inc=1, device_id=(grp, peer), device_id_type=MESH)
    for other in (grp_x, grp_y):
        pl.semaphore_signal(barrier, inc=1, device_id=(other, me), device_id_type=MESH)
    pl.semaphore_wait(barrier, len(peers) + 1)


def remote(src, dst, send_sem, recv_sem, device):
    return pltpu.make_async_remote_copy(
        src_ref=src, dst_ref=dst, send_sem=send_sem, recv_sem=recv_sem,
        device_id=device, device_id_type=MESH,
    )


def dispatch_kernel(shards, rows_ref, out_ref, z_sem, x_sem, y_sem, fx_sem, fy_sem, own_sem):
    grp, me, grp_x, grp_y, _, peers = places(shards)
    greet(grp, me, grp_x, grp_y, peers)
    own = pltpu.make_async_copy(rows_ref.at[:, me], out_ref.at[:, grp, me], own_sem)
    own.start()

    def to_neighbours(k):
        src = rows_ref.at[:, me] if k == 0 else out_ref.at[:, grp, peers[k]]
        dst = out_ref.at[:, grp, peers[k]]
        pair = (
            remote(src, dst, x_sem.at[0, k], x_sem.at[1, k], (grp_x, me)),
            remote(src, dst, y_sem.at[0, k], y_sem.at[1, k], (grp_y, me)),
        )
        for copy in pair:
            copy.start()
        return pair

    def forward(k):
        direct[k][0].wait_recv()
        src = out_ref.at[0, grp_x, peers[k]]
        first = remote(src, src, fy_sem.at[0, k], fy_sem.at[1, k], (grp_y, me))
        first.start()
        direct[k][1].wait_recv()
        src = out_ref.at[1, grp_y, peers[k]]
        second = remote(src, src, fx_sem.at[0, k], fx_sem.at[1, k], (grp_x, me))
        second.start()
        return first, second

    direct = [to_neighbours(0)]
    over_z = [None]
    for k in range(1, shards):
        copy = remote(
            rows_ref.at[:, peers[k]], out_ref.at[:, grp, me],
            z_sem.at[0, k], z_sem.at[1, k], (grp, peers[k]),
        )
        copy.start()
        over_z.append(copy)
    passed = []
    lag = 2
    for k in range(1, shards):
        over_z[k].wait_recv()
        direct.append(to_neighbours(k))
        if k >= lag:
            passed.append(forward(k - lag))
    for k in range(shards - lag, shards):
        passed.append(forward(k))
    own.wait()
    for copy in over_z[1:]:
        copy.wait_send()
    for pair in direct:
        for copy in pair:
            copy.wait_send()
    for pair in passed:
        for copy in pair:
            copy.wait()


def dispatch(rows, groups):
    kinds, shards, depth, width = rows.shape
    sem = pltpu.SemaphoreType.DMA((2, shards))
    return pl.pallas_call(
        functools.partial(dispatch_kernel, shards),
        out_shape=jax.ShapeDtypeStruct((kinds, groups, shards, depth, width), rows.dtype),
        in_specs=[pl.BlockSpec(memory_space=pl.ANY)],
        out_specs=pl.BlockSpec(memory_space=pl.ANY),
        scratch_shapes=[sem, sem, sem, sem, sem, pltpu.SemaphoreType.DMA],
        compiler_params=pltpu.CompilerParams(collective_id=0, has_side_effects=True),
        name="dispatch",
    )(rows)


def experts_kernel(perm_ref, arrived_ref, wg_ref, wu_ref, wd_ref, gg_ref, gu_ref, gd_ref, back_ref, rows):
    step = pl.program_id(0)
    last = pl.num_programs(0) - 1
    kinds, groups, shards, depth, width = arrived_ref.shape
    tiles = depth // TILE
    half = groups // 2
    block = half * shards * TILE
    share = half * shards * CAP
    spare = half * shards
    odd = PER_TILE * tiles
    chunk = min(512, width)

    def spots(tile, side):
        spans = [(tile * PER_TILE + j, side * share, share) for j in range(PER_TILE)]
        return spans + [(odd, (2 * tile + side) * spare, spare)]

    @pl.when(step == 0)
    def _():
        def columns(c, _):
            cols = pl.ds(pl.multiple_of(c * chunk, chunk), chunk)
            for kind in range(kinds):
                for tile in range(tiles):
                    for side in range(2):
                        part = arrived_ref[
                            kind, side * half:(side + 1) * half, :, tile * TILE:(tile + 1) * TILE, cols
                        ].reshape(block, chunk)
                        sorted_part = jnp.dot(
                            perm_ref[...], part, preferred_element_type=F32
                        ).astype(BF16)
                        at = 0
                        for expert, start, size in spots(tile, side):
                            rows[kind, expert, start:start + size, cols] = sorted_part[at:at + size]
                            at += size
            return 0

        lax.fori_loop(0, width // chunk, columns, 0)

    by_last = (((1,), (1,)), ((), ()))
    by_first = (((0,), (0,)), ((), ()))
    x = rows[0, step]
    gated = rows[1, step]
    wg, wu = wg_ref[0], wu_ref[0]
    pre_gate = lax.dot_general(x, wg, by_last, preferred_element_type=F32)
    pre_up = lax.dot_general(x, wu, by_last, preferred_element_type=F32)
    act_grad = lax.dot_general(gated, wd_ref[0], by_last, preferred_element_type=F32)
    act_val, act_slope = silu_parts(pre_gate)
    activation = (act_val * pre_up).astype(BF16)
    gate_grad = (act_grad * pre_up * act_slope).astype(BF16)
    up_grad = (act_grad * act_val).astype(BF16)
    gd_ref[0] = lax.dot_general(activation, gated, by_first, preferred_element_type=F32).astype(BF16)
    gg_ref[0] = lax.dot_general(gate_grad, x, by_first, preferred_element_type=F32).astype(BF16)
    gu_ref[0] = lax.dot_general(up_grad, x, by_first, preferred_element_type=F32).astype(BF16)
    hidden = jnp.dot(gate_grad, wg, preferred_element_type=F32) + jnp.dot(
        up_grad, wu, preferred_element_type=F32
    )
    rows[0, step] = hidden.astype(BF16)

    @pl.when(step == last)
    def _():
        def columns(c, _):
            cols = pl.ds(pl.multiple_of(c * chunk, chunk), chunk)
            for tile in range(tiles):
                for side in range(2):
                    part = jnp.concatenate(
                        [rows[0, expert, start:start + size, cols] for expert, start, size in spots(tile, side)],
                        axis=0,
                    )
                    back = lax.dot_general(
                        perm_ref[...], part, by_first, preferred_element_type=F32
                    ).astype(BF16)
                    back_ref[
                        side * half:(side + 1) * half, :, tile * TILE:(tile + 1) * TILE, cols
                    ] = back.reshape(half, shards, TILE, chunk)
            return 0

        lax.fori_loop(0, width // chunk, columns, 0)


def sort_matrix(sources):
    taken = jnp.arange(sources * TILE, dtype=jnp.int32)
    source, place = taken // TILE, taken % TILE
    goes = jnp.where(
        place < PER_TILE * CAP,
        place // CAP * (sources * CAP) + source * CAP + place % CAP,
        PER_TILE * CAP * sources + source,
    )
    return (goes[None, :] == taken[:, None]).astype(BF16)


def experts(arrived, w_gate, w_up, w_down):
    kinds, groups, shards, depth, width = arrived.shape
    count, hidden, _ = w_gate.shape
    perm = sort_matrix(groups // 2 * shards)
    weight = pl.BlockSpec((1, hidden, width), lambda e: (e, 0, 0))
    grad = jax.ShapeDtypeStruct(w_gate.shape, BF16)
    row_count = groups * shards * CAP
    return pl.pallas_call(
        experts_kernel,
        grid=(count,),
        out_shape=(grad, grad, grad, jax.ShapeDtypeStruct(arrived.shape[1:], BF16)),
        in_specs=[
            pl.BlockSpec(perm.shape, lambda e: (0, 0)),
            pl.BlockSpec(arrived.shape, lambda e: (0, 0, 0, 0, 0), pipeline_mode=pl.Buffered(1)),
            weight,
            weight,
            weight,
        ],
        out_specs=(weight, weight, weight, pl.BlockSpec(arrived.shape[1:], lambda e: (0, 0, 0, 0))),
        scratch_shapes=[pltpu.VMEM((kinds, count, row_count, width), BF16)],
        compiler_params=pltpu.CompilerParams(vmem_limit_bytes=60 * 1024 * 1024),
        cost_estimate=pl.CostEstimate(
            flops=16 * count * row_count * hidden * width,
            bytes_accessed=12 * count * hidden * width + 6 * groups * shards * depth * width,
            transcendentals=count * row_count * hidden,
        ),
        name="experts",
    )(perm, arrived, w_gate, w_up, w_down)


def combine_kernel(shards, part_ref, out_ref, from_x, from_y, mid_x, mid_y, end_x, end_y, done,
                   x_sem, y_sem, x2_sem, y2_sem, z_sem):
    grp, me, grp_x, grp_y, grp_d, peers = places(shards)
    width = part_ref.shape[-1]
    low, high = pl.ds(0, width // 2), pl.ds(width // 2, width // 2)
    greet(grp, me, grp_x, grp_y, peers)
    order = list(range(shards - 1, -1, -1))

    def first(k):
        q = peers[k]
        out = []
        for j, target in enumerate((grp_d, grp_x)):
            out.append(remote(
                part_ref.at[target, q, :, low], from_x.at[q, 1 - j],
                x_sem.at[0, k, j], x_sem.at[1, k, j], (grp_x, me),
            ))
        for j, target in enumerate((grp_d, grp_y)):
            out.append(remote(
                part_ref.at[target, q, :, high], from_y.at[q, 1 - j],
                y_sem.at[0, k, j], y_sem.at[1, k, j], (grp_y, me),
            ))
        for copy in (out[0], out[2], out[1], out[3]):
            copy.start()
        return out

    def second(k):
        q = peers[k]
        starts[k][0].wait_recv()
        mid_x[q] = (part_ref[grp_y, q, :, low].astype(F32) + from_x[q, 1].astype(F32)).astype(BF16)
        to_y = remote(mid_x.at[q], end_y.at[q], y2_sem.at[0, k], y2_sem.at[1, k], (grp_y, me))
        to_y.start()
        starts[k][2].wait_recv()
        mid_y[q] = (part_ref[grp_x, q, :, high].astype(F32) + from_y[q, 1].astype(F32)).astype(BF16)
        to_x = remote(mid_y.at[q], end_x.at[q], x2_sem.at[0, k], x2_sem.at[1, k], (grp_x, me))
        to_x.start()
        return to_y, to_x

    def third(k):
        q = peers[k]
        starts[k][1].wait_recv()
        middles[k][0].wait_recv()
        done[q, :, low] = (
            part_ref[grp, q, :, low].astype(F32) + from_x[q, 0].astype(F32) + end_y[q].astype(F32)
        ).astype(BF16)
        starts[k][3].wait_recv()
        middles[k][1].wait_recv()
        done[q, :, high] = (
            part_ref[grp, q, :, high].astype(F32) + from_y[q, 0].astype(F32) + end_x[q].astype(F32)
        ).astype(BF16)
        if k == 0:
            out_ref[me] = done[me]
            return None
        copy = remote(done.at[q], out_ref.at[me], z_sem.at[0, k], z_sem.at[1, k], (grp, q))
        copy.start()
        return copy

    starts, middles, returns = {}, {}, []
    ahead, lag = 2, 1
    for i in range(shards + ahead + lag):
        if i < shards:
            starts[order[i]] = first(order[i])
        if 0 <= i - ahead < shards:
            middles[order[i - ahead]] = second(order[i - ahead])
        if 0 <= i - ahead - lag:
            returns.append(third(order[i - ahead - lag]))
    for k in order:
        for copy in starts[k]:
            copy.wait_send()
        for copy in middles[k]:
            copy.wait_send()
    for copy in returns:
        if copy is not None:
            copy.wait()


def combine(parts):
    groups, shards, depth, width = parts.shape
    half = (shards, depth, width // 2)
    pair = (shards, 2, depth, width // 2)
    return pl.pallas_call(
        functools.partial(combine_kernel, shards),
        out_shape=jax.ShapeDtypeStruct((shards, depth, width), parts.dtype),
        in_specs=[pl.BlockSpec(memory_space=pltpu.VMEM)],
        out_specs=pl.BlockSpec(memory_space=pltpu.VMEM),
        scratch_shapes=[
            pltpu.VMEM(pair, BF16), pltpu.VMEM(pair, BF16),
            pltpu.VMEM(half, BF16), pltpu.VMEM(half, BF16),
            pltpu.VMEM(half, BF16), pltpu.VMEM(half, BF16),
            pltpu.VMEM((shards, depth, width), BF16),
            pltpu.SemaphoreType.DMA((2, shards, 2)), pltpu.SemaphoreType.DMA((2, shards, 2)),
            pltpu.SemaphoreType.DMA((2, shards)), pltpu.SemaphoreType.DMA((2, shards)),
            pltpu.SemaphoreType.DMA((2, shards)),
        ],
        compiler_params=pltpu.CompilerParams(
            collective_id=1, has_side_effects=True, vmem_limit_bytes=48 * 1024 * 1024
        ),
        name="combine",
    )(parts)


def body(moe_input, out_grad, expert_ids, gate_weights, w_gate, w_up, w_down):
    contract_rows = (((0,), (0,)), ((), ()))
    shards = lax.axis_size("shard")
    groups = lax.axis_size("grp")
    per_device = w_gate.shape[0]
    tokens_here, model_width = moe_input.shape
    depth = per_device * CAP
    tiles = depth // TILE
    flat_ids = expert_ids.reshape(tokens_here * TOP)
    matches = (flat_ids[:, None] == jnp.arange(EXPERTS, dtype=jnp.int32)[None, :]).astype(jnp.int32)
    rank_of = jnp.sum((jnp.cumsum(matches, axis=0) - matches) * matches, axis=1)
    local = flat_ids % per_device
    odd = PER_TILE * tiles
    place = jnp.where(
        local < odd,
        local // PER_TILE * TILE + local % PER_TILE * CAP + rank_of,
        rank_of * TILE + PER_TILE * CAP,
    )
    slot_of = (flat_ids // per_device * depth + place).reshape(tokens_here, TOP)
    slots = jnp.arange(EXPERTS * CAP, dtype=jnp.int32)
    chosen = slot_of[:, :, None] == slots[None, None, :]
    token_map = jnp.any(chosen, axis=1).astype(BF16)
    gate_map = jnp.sum(
        jnp.where(chosen, gate_weights.astype(F32)[:, :, None], 0.0), axis=1
    ).astype(BF16)
    input_slots = lax.dot_general(token_map, moe_input, contract_rows, preferred_element_type=F32)
    gated_slots = lax.dot_general(gate_map, out_grad, contract_rows, preferred_element_type=F32)
    sent = jnp.stack([input_slots.astype(BF16), gated_slots.astype(BF16)])
    arrived = dispatch(sent.reshape(2, shards, depth, model_width), groups)
    grad_gate, grad_up, grad_down, parts = experts(arrived, w_gate, w_up, w_down)
    returned = combine(parts).reshape(shards * depth, model_width)
    moe_grad = jnp.dot(token_map, returned, preferred_element_type=F32)
    input_grad = (out_grad.astype(F32) + moe_grad).astype(BF16)
    return (input_grad, grad_gate, grad_up, grad_down)


def plain_slot_maps(ids_here, per_device, shards):
    tokens_here = ids_here.shape[0]
    flat_ids = ids_here.reshape(tokens_here * TOP)
    matches = (flat_ids[:, None] == jnp.arange(EXPERTS, dtype=jnp.int32)[None, :]).astype(jnp.int32)
    rank_of = jnp.sum((jnp.cumsum(matches, axis=0) - matches) * matches, axis=1)
    slot_of = flat_ids % per_device * (shards * CAP) + flat_ids // per_device * CAP + rank_of
    return (slot_of[:, None] == jnp.arange(EXPERTS * CAP, dtype=jnp.int32)[None, :]).astype(F32)


def plain_body(moe_input, out_grad, expert_ids, gate_weights, w_gate, w_up, w_down):
    contract_rows = (((0,), (0,)), ((), ()))
    shards = lax.axis_size("shard")
    groups = lax.axis_size("grp")
    per_device = w_gate.shape[0]
    tokens_here, model_width = moe_input.shape
    slot_total = EXPERTS * CAP
    chosen = plain_slot_maps(expert_ids, per_device, shards).reshape(tokens_here, TOP, slot_total)
    token_map = jnp.sum(chosen, axis=1)
    gate_map = jnp.sum(chosen * gate_weights.astype(F32)[:, :, None], axis=1).astype(BF16)
    slot_shape = (per_device, shards, CAP, model_width)
    row_count = groups * shards * CAP

    def send(mapping, rows):
        slots = lax.dot_general(mapping, rows, contract_rows, preferred_element_type=F32).astype(BF16)
        arrived = lax.all_to_all(
            slots.reshape(slot_shape), "shard", split_axis=1, concat_axis=1, tiled=True
        )
        gathered = lax.all_gather(arrived, "grp", axis=1, tiled=True)
        return gathered.reshape(per_device, row_count, model_width)

    inputs = send(token_map.astype(BF16), moe_input)
    gated = send(gate_map, out_grad)
    pre_gate = jnp.einsum("efd,erd->efr", w_gate, inputs, preferred_element_type=F32)
    pre_up = jnp.einsum("efd,erd->efr", w_up, inputs, preferred_element_type=F32)
    act_val, act_slope = silu_parts(pre_gate)
    activation = (act_val * pre_up).astype(BF16)
    act_grad = jnp.einsum("efd,erd->efr", w_down, gated, preferred_element_type=F32)
    gate_grad = (act_grad * pre_up * act_slope).astype(BF16)
    up_grad = (act_grad * act_val).astype(BF16)
    grad_down = jnp.einsum("efr,erd->efd", activation, gated, preferred_element_type=F32).astype(BF16)
    grad_gate = jnp.einsum("efr,erd->efd", gate_grad, inputs, preferred_element_type=F32).astype(BF16)
    grad_up = jnp.einsum("efr,erd->efd", up_grad, inputs, preferred_element_type=F32).astype(BF16)
    hidden_part = jnp.einsum(
        "efr,efd->erd", gate_grad, w_gate, preferred_element_type=F32
    ) + jnp.einsum("efr,efd->erd", up_grad, w_up, preferred_element_type=F32)
    hidden_part = hidden_part.reshape(per_device, groups, shards, CAP, model_width)
    own_part = lax.psum_scatter(hidden_part, "grp", scatter_dimension=1, tiled=True)
    returned = lax.all_to_all(own_part, "shard", split_axis=2, concat_axis=2, tiled=True)
    moe_grad = jnp.einsum(
        "tesc,escd->td",
        token_map.reshape(tokens_here, per_device, shards, CAP),
        returned.reshape(per_device, shards, CAP, model_width),
        precision=lax.Precision.HIGHEST,
        preferred_element_type=F32,
    )
    input_grad = (out_grad.astype(F32) + moe_grad).astype(BF16)
    return (input_grad, grad_gate, grad_up, grad_down)


def solution(mesh):
    groups, shards = mesh.shape["grp"], mesh.shape["shard"]
    per_device = EXPERTS // shards
    tiles = per_device * CAP // TILE
    fits = (
        groups == 4
        and shards & (shards - 1) == 0
        and per_device * CAP == tiles * TILE
        and per_device == PER_TILE * tiles + 1
        and tiles == CAP
    )
    tokens = P(("grp", "shard"), None)
    weights = P("shard", "grp", None)
    return jax.shard_map(
        body if fits else plain_body,
        mesh=mesh,
        in_specs=(tokens, tokens, tokens, tokens, weights, weights, weights),
        out_specs=(tokens, weights, weights, weights),
        check_vma=False,
    )
```

```python
import functools

import jax
import jax.numpy as jnp
from jax import lax
from jax.experimental import pallas as pl
from jax.experimental.pallas import tpu as pltpu
from jax.sharding import PartitionSpec as P

EXPERTS = 128
TOP = 2
CAP = 3
TILE = 16
PER_TILE = TILE // CAP
MESH = pl.DeviceIdType.MESH
F32 = jnp.float32
BF16 = jnp.bfloat16


def silu_parts(pre_act):
    sigmoid_val = jax.nn.sigmoid(pre_act)
    return (pre_act * sigmoid_val, sigmoid_val * (1.0 + pre_act * (1.0 - sigmoid_val)))


def flip(index, bits):
    bit = 1
    while bit <= bits:
        if bits & bit:
            index = index + bit * (1 - 2 * ((index // bit) % 2))
        bit *= 2
    return index


def places(shards):
    grp, me = lax.axis_index("grp"), lax.axis_index("shard")
    peers = [flip(me, k) for k in range(shards)]
    return grp, me, flip(grp, 1), flip(grp, 2), flip(grp, 3), peers


def greet(grp, me, grp_x, grp_y, peers):
    barrier = pltpu.get_barrier_semaphore()
    for peer in peers[1:]:
        pl.semaphore_signal(barrier, inc=1, device_id=(grp, peer), device_id_type=MESH)
    for other in (grp_x, grp_y):
        pl.semaphore_signal(barrier, inc=1, device_id=(other, me), device_id_type=MESH)
    pl.semaphore_wait(barrier, len(peers) + 1)


def remote(src, dst, send_sem, recv_sem, device):
    return pltpu.make_async_remote_copy(
        src_ref=src, dst_ref=dst, send_sem=send_sem, recv_sem=recv_sem,
        device_id=device, device_id_type=MESH,
    )


def exchange_kernel(order, rows_ref, wg_ref, wu_ref, wd_ref, perm_ref, sorted_ref, acts_ref, out_ref,
                    arrived, rows, hidden, parts, weights, from_x, from_y, mid_x, mid_y, end_x, end_y, done,
                    zs, xs, ys, fxs, fys, cx, cy, cx2, cy2, cz, w_sem, own_sem, sorted_sem):
    shards = len(order)
    grp, me, grp_x, grp_y, _, by_flip = places(shards)
    peers = [by_flip[k] for k in order]
    kinds, groups, _, depth, width = arrived.shape
    count = rows.shape[1]
    tiles = depth // TILE
    half = shards // 2
    block = groups * half * TILE
    share = groups * half * CAP
    spare = groups * half
    odd = PER_TILE * tiles
    chunk = min(512, width)
    low, high = pl.ds(0, width // 2), pl.ds(width // 2, width // 2)
    by_last = (((1,), (1,)), ((), ()))
    by_first = (((0,), (0,)), ((), ()))
    on_x, on_y = (grp_x, me), (grp_y, me)

    def weight_copies(e, slot):
        return [
            pltpu.make_async_copy(ref.at[e], weights.at[j, slot], w_sem.at[j, slot])
            for j, ref in enumerate((wg_ref, wu_ref, wd_ref))
        ]

    def to_neighbours(i):
        src = rows_ref.at[:, me] if i == 0 else arrived.at[:, 0, i]
        pair = (
            remote(src, arrived.at[:, 1, i], xs.at[0, i], xs.at[1, i], on_x),
            remote(src, arrived.at[:, 2, i], ys.at[0, i], ys.at[1, i], on_y),
        )
        for copy in pair:
            copy.start()
        direct[i] = pair

    def forward(i):
        direct[i][0].wait_recv()
        first = remote(arrived.at[0, 1, i], arrived.at[0, 3, i], fys.at[0, i], fys.at[1, i], on_y)
        first.start()
        direct[i][1].wait_recv()
        second = remote(arrived.at[1, 2, i], arrived.at[1, 3, i], fxs.at[0, i], fxs.at[1, i], on_x)
        second.start()
        passed[i] = (first, second)

    def relay(i):
        over_z[i].wait_recv()
        to_neighbours(i)
        if i >= 2:
            forward(i - 2)

    def sort(side):
        for i in range(side * half, (side + 1) * half):
            for copy in passed[i]:
                copy.wait_recv()

        def columns(c, _):
            cols = pl.ds(pl.multiple_of(c * chunk, chunk), chunk)
            for kind in range(kinds):
                for tile in range(tiles):
                    part = arrived[
                        kind, :, side * half:(side + 1) * half, tile * TILE:(tile + 1) * TILE, cols
                    ].reshape(block, chunk)
                    placed = jnp.dot(perm_ref[...], part, preferred_element_type=F32).astype(BF16)
                    base = side * share
                    for j in range(PER_TILE):
                        rows[kind, tile * PER_TILE + j, base:base + share, cols] = placed[j * share:(j + 1) * share]
                    base += tile * spare
                    rows[kind, odd, base:base + spare, cols] = placed[PER_TILE * share:]
            return 0

        lax.fori_loop(0, width // chunk, columns, 0)
        span = pl.ds(side * share, share)
        copy = pltpu.make_async_copy(rows.at[:, :, span], sorted_ref.at[:, :, span], sorted_sem.at[side])
        copy.start()
        written.append(copy)

    def experts(side, begin, end):
        span = pl.ds(side * share, share)

        def one(e, _):
            slot = e % 2

            def fetch():
                for copy in weight_copies((e + 1) % count, 1 - slot):
                    copy.start()

            if side == 0:
                fetch()
            else:
                pl.when(e + 1 < count)(fetch)
            for copy in weight_copies(e, slot):
                copy.wait()
            x = rows[0, e, span]
            gated = rows[1, e, span]
            wg, wu = weights[0, slot], weights[1, slot]
            pre_gate = lax.dot_general(x, wg, by_last, preferred_element_type=F32)
            pre_up = lax.dot_general(x, wu, by_last, preferred_element_type=F32)
            act_grad = lax.dot_general(gated, weights[2, slot], by_last, preferred_element_type=F32)
            act_val, act_slope = silu_parts(pre_gate)
            gate_grad = (act_grad * pre_up * act_slope).astype(BF16)
            up_grad = (act_grad * act_val).astype(BF16)
            acts_ref[0, e, span] = (act_val * pre_up).astype(BF16)
            acts_ref[1, e, span] = gate_grad
            acts_ref[2, e, span] = up_grad
            hidden[e] = (
                jnp.dot(gate_grad, wg, preferred_element_type=F32)
                + jnp.dot(up_grad, wu, preferred_element_type=F32)
            ).astype(BF16)
            return 0

        lax.fori_loop(begin, end, one, 0)

    def unsort(side):
        def columns(c, _):
            cols = pl.ds(pl.multiple_of(c * chunk, chunk), chunk)
            for tile in range(tiles):
                spans = [hidden[tile * PER_TILE + j, :, cols] for j in range(PER_TILE)]
                spans.append(hidden[odd, tile * spare:(tile + 1) * spare, cols])
                back = lax.dot_general(
                    perm_ref[...], jnp.concatenate(spans, axis=0), by_first, preferred_element_type=F32
                ).astype(BF16)
                parts[
                    :, side * half:(side + 1) * half, tile * TILE:(tile + 1) * TILE, cols
                ] = back.reshape(groups, half, TILE, chunk)
            return 0

        lax.fori_loop(0, width // chunk, columns, 0)

    def first(i):
        out = []
        for j, rel in enumerate((3, 1)):
            out.append(remote(
                parts.at[rel, i, :, low], from_x.at[i, 1 - j], cx.at[0, i, j], cx.at[1, i, j], on_x
            ))
        for j, rel in enumerate((3, 2)):
            out.append(remote(
                parts.at[rel, i, :, high], from_y.at[i, 1 - j], cy.at[0, i, j], cy.at[1, i, j], on_y
            ))
        for copy in (out[0], out[2], out[1], out[3]):
            copy.start()
        starts[i] = out

    def second(i):
        starts[i][0].wait_recv()
        mid_x[i] = (parts[2, i, :, low].astype(F32) + from_x[i, 1].astype(F32)).astype(BF16)
        to_y = remote(mid_x.at[i], end_y.at[i], cy2.at[0, i], cy2.at[1, i], on_y)
        to_y.start()
        starts[i][2].wait_recv()
        mid_y[i] = (parts[1, i, :, high].astype(F32) + from_y[i, 1].astype(F32)).astype(BF16)
        to_x = remote(mid_y.at[i], end_x.at[i], cx2.at[0, i], cx2.at[1, i], on_x)
        to_x.start()
        middles[i] = (to_y, to_x)

    def third(i):
        starts[i][1].wait_recv()
        middles[i][0].wait_recv()
        done[i, :, low] = (
            parts[0, i, :, low].astype(F32) + from_x[i, 0].astype(F32) + end_y[i].astype(F32)
        ).astype(BF16)
        starts[i][3].wait_recv()
        middles[i][1].wait_recv()
        done[i, :, high] = (
            parts[0, i, :, high].astype(F32) + from_y[i, 0].astype(F32) + end_x[i].astype(F32)
        ).astype(BF16)
        if i == 0:
            out_ref[me] = done[0]
            return
        copy = remote(done.at[i], out_ref.at[me], cz.at[0, i], cz.at[1, i], (grp, peers[i]))
        copy.start()
        returns.append(copy)

    direct, over_z, passed, starts, middles = {}, {}, {}, {}, {}
    returns, written = [], []
    for copy in weight_copies(0, 0):
        copy.start()
    greet(grp, me, grp_x, grp_y, by_flip)
    own = pltpu.make_async_copy(rows_ref.at[:, me], arrived.at[:, 0, 0], own_sem)
    own.start()
    to_neighbours(0)
    for i in range(1, shards):
        over_z[i] = remote(
            rows_ref.at[:, peers[i]], arrived.at[:, 0, i], zs.at[0, i], zs.at[1, i], (grp, peers[i])
        )
        over_z[i].start()
    for i in range(1, half + 2):
        relay(i)
    own.wait()
    sort(0)
    steps = half - 2
    for j, i in enumerate(range(half + 2, shards)):
        relay(i)
        experts(0, j * count // steps, (j + 1) * count // steps)
    forward(shards - 2)
    unsort(0)
    turn = list(range(half // 2, half)) + list(range(half // 2 - 1, -1, -1))
    first(turn[0])
    first(turn[1])
    forward(shards - 1)
    for i in turn[2:]:
        first(i)
    sort(1)
    for j, i in enumerate(turn):
        experts(1, j * count // half, (j + 1) * count // half)
        second(i)
        if j > 0:
            third(turn[j - 1])
    unsort(1)
    later = [half + i for i in turn]
    ahead = 2
    for j in range(half + ahead + 1):
        if j < half:
            first(later[j])
        if j == 1:
            third(turn[-1])
        if 0 <= j - ahead < half:
            second(later[j - ahead])
        if 0 <= j - ahead - 1:
            third(later[j - ahead - 1])
    for i in range(shards):
        if i > 0:
            over_z[i].wait_send()
        for copy in direct[i] + passed[i] + tuple(starts[i]) + middles[i]:
            copy.wait_send()
    for copy in written:
        copy.wait()
    for copy in returns:
        copy.wait()


def sort_matrix(sources):
    taken = jnp.arange(sources * TILE, dtype=jnp.int32)
    source, place = taken // TILE, taken % TILE
    goes = jnp.where(
        place < PER_TILE * CAP,
        place // CAP * (sources * CAP) + source * CAP + place % CAP,
        PER_TILE * CAP * sources + source,
    )
    return (goes[None, :] == taken[:, None]).astype(BF16)


def exchange(sent, w_gate, w_up, w_down, groups):
    kinds, shards, depth, width = sent.shape
    count, units, _ = w_gate.shape
    row_count = groups * shards * CAP
    order = sorted(range(shards), key=lambda k: (k // 2 % 2, k))
    perm = sort_matrix(groups * shards // 2)
    half = pltpu.VMEM((shards, depth, width // 2), BF16)
    pair = pltpu.VMEM((shards, 2, depth, width // 2), BF16)
    sem = pltpu.SemaphoreType.DMA((2, shards))
    sem_pair = pltpu.SemaphoreType.DMA((2, shards, 2))
    anywhere = pl.BlockSpec(memory_space=pl.ANY)
    near = pl.BlockSpec(memory_space=pltpu.VMEM)
    return pl.pallas_call(
        functools.partial(exchange_kernel, order),
        out_shape=(
            jax.ShapeDtypeStruct((kinds, count, row_count, width), BF16),
            jax.ShapeDtypeStruct((3, count, row_count, units), BF16),
            jax.ShapeDtypeStruct((shards, depth, width), BF16),
        ),
        in_specs=[anywhere, anywhere, anywhere, anywhere, near],
        out_specs=(anywhere, near, near),
        scratch_shapes=[
            pltpu.VMEM((kinds, groups, shards, depth, width), BF16),
            pltpu.VMEM((kinds, count, row_count, width), BF16),
            pltpu.VMEM((count, row_count // 2, width), BF16),
            pltpu.VMEM((groups, shards, depth, width), BF16),
            pltpu.VMEM((3, 2, units, width), BF16),
            pair, pair, half, half, half, half,
            pltpu.VMEM((shards, depth, width), BF16),
            sem, sem, sem, sem, sem, sem_pair, sem_pair, sem, sem, sem,
            pltpu.SemaphoreType.DMA((3, 2)),
            pltpu.SemaphoreType.DMA,
            pltpu.SemaphoreType.DMA((2,)),
        ],
        compiler_params=pltpu.CompilerParams(
            collective_id=0, has_side_effects=True, vmem_limit_bytes=60 * 1024 * 1024
        ),
        name="exchange",
    )(sent, w_gate, w_up, w_down, perm)


def grads_kernel(rows_ref, acts_ref, gg_ref, gu_ref, gd_ref):
    by_first = (((0,), (0,)), ((), ()))
    x, gated = rows_ref[0, 0], rows_ref[1, 0]
    for ref, j, side in ((gd_ref, 0, gated), (gg_ref, 1, x), (gu_ref, 2, x)):
        ref[0] = lax.dot_general(acts_ref[j, 0], side, by_first, preferred_element_type=F32).astype(BF16)


def grads(rows, acts):
    kinds, count, row_count, width = rows.shape
    units = acts.shape[-1]
    grad = jax.ShapeDtypeStruct((count, units, width), BF16)
    out = pl.BlockSpec((1, units, width), lambda e: (e, 0, 0))
    return pl.pallas_call(
        grads_kernel,
        grid=(count,),
        out_shape=(grad, grad, grad),
        in_specs=[
            pl.BlockSpec((kinds, 1, row_count, width), lambda e: (0, e, 0, 0)),
            pl.BlockSpec((3, 1, row_count, units), lambda e: (0, e, 0, 0)),
        ],
        out_specs=(out, out, out),
        compiler_params=pltpu.CompilerParams(vmem_limit_bytes=32 * 1024 * 1024),
        name="grads",
    )(rows, acts)


def body(moe_input, out_grad, expert_ids, gate_weights, w_gate, w_up, w_down):
    contract_rows = (((0,), (0,)), ((), ()))
    shards = lax.axis_size("shard")
    groups = lax.axis_size("grp")
    per_device = w_gate.shape[0]
    tokens_here, model_width = moe_input.shape
    depth = per_device * CAP
    tiles = depth // TILE
    flat_ids = expert_ids.reshape(tokens_here * TOP)
    matches = (flat_ids[:, None] == jnp.arange(EXPERTS, dtype=jnp.int32)[None, :]).astype(jnp.int32)
    rank_of = jnp.sum((jnp.cumsum(matches, axis=0) - matches) * matches, axis=1)
    local = flat_ids % per_device
    odd = PER_TILE * tiles
    place = jnp.where(
        local < odd,
        local // PER_TILE * TILE + local % PER_TILE * CAP + rank_of,
        rank_of * TILE + PER_TILE * CAP,
    )
    slot_of = (flat_ids // per_device * depth + place).reshape(tokens_here, TOP)
    slots = jnp.arange(EXPERTS * CAP, dtype=jnp.int32)
    chosen = slot_of[:, :, None] == slots[None, None, :]
    token_map = jnp.any(chosen, axis=1).astype(BF16)
    gate_map = jnp.sum(
        jnp.where(chosen, gate_weights.astype(F32)[:, :, None], 0.0), axis=1
    ).astype(BF16)
    input_slots = lax.dot_general(token_map, moe_input, contract_rows, preferred_element_type=F32)
    gated_slots = lax.dot_general(gate_map, out_grad, contract_rows, preferred_element_type=F32)
    sent = jnp.stack([input_slots.astype(BF16), gated_slots.astype(BF16)])
    sorted_rows, acts, returned = exchange(
        sent.reshape(2, shards, depth, model_width), w_gate, w_up, w_down, groups
    )
    grad_gate, grad_up, grad_down = grads(sorted_rows, acts)
    returned = returned.reshape(shards * depth, model_width)
    moe_grad = jnp.dot(token_map, returned, preferred_element_type=F32)
    input_grad = (out_grad.astype(F32) + moe_grad).astype(BF16)
    return (input_grad, grad_gate, grad_up, grad_down)


def plain_slot_maps(ids_here, per_device, shards):
    tokens_here = ids_here.shape[0]
    flat_ids = ids_here.reshape(tokens_here * TOP)
    matches = (flat_ids[:, None] == jnp.arange(EXPERTS, dtype=jnp.int32)[None, :]).astype(jnp.int32)
    rank_of = jnp.sum((jnp.cumsum(matches, axis=0) - matches) * matches, axis=1)
    slot_of = flat_ids % per_device * (shards * CAP) + flat_ids // per_device * CAP + rank_of
    return (slot_of[:, None] == jnp.arange(EXPERTS * CAP, dtype=jnp.int32)[None, :]).astype(F32)


def plain_body(moe_input, out_grad, expert_ids, gate_weights, w_gate, w_up, w_down):
    contract_rows = (((0,), (0,)), ((), ()))
    shards = lax.axis_size("shard")
    groups = lax.axis_size("grp")
    per_device = w_gate.shape[0]
    tokens_here, model_width = moe_input.shape
    slot_total = EXPERTS * CAP
    chosen = plain_slot_maps(expert_ids, per_device, shards).reshape(tokens_here, TOP, slot_total)
    token_map = jnp.sum(chosen, axis=1)
    gate_map = jnp.sum(chosen * gate_weights.astype(F32)[:, :, None], axis=1).astype(BF16)
    slot_shape = (per_device, shards, CAP, model_width)
    row_count = groups * shards * CAP

    def send(mapping, rows):
        slots = lax.dot_general(mapping, rows, contract_rows, preferred_element_type=F32).astype(BF16)
        arrived = lax.all_to_all(
            slots.reshape(slot_shape), "shard", split_axis=1, concat_axis=1, tiled=True
        )
        gathered = lax.all_gather(arrived, "grp", axis=1, tiled=True)
        return gathered.reshape(per_device, row_count, model_width)

    inputs = send(token_map.astype(BF16), moe_input)
    gated = send(gate_map, out_grad)
    pre_gate = jnp.einsum("efd,erd->efr", w_gate, inputs, preferred_element_type=F32)
    pre_up = jnp.einsum("efd,erd->efr", w_up, inputs, preferred_element_type=F32)
    act_val, act_slope = silu_parts(pre_gate)
    activation = (act_val * pre_up).astype(BF16)
    act_grad = jnp.einsum("efd,erd->efr", w_down, gated, preferred_element_type=F32)
    gate_grad = (act_grad * pre_up * act_slope).astype(BF16)
    up_grad = (act_grad * act_val).astype(BF16)
    grad_down = jnp.einsum("efr,erd->efd", activation, gated, preferred_element_type=F32).astype(BF16)
    grad_gate = jnp.einsum("efr,erd->efd", gate_grad, inputs, preferred_element_type=F32).astype(BF16)
    grad_up = jnp.einsum("efr,erd->efd", up_grad, inputs, preferred_element_type=F32).astype(BF16)
    hidden_part = jnp.einsum(
        "efr,efd->erd", gate_grad, w_gate, preferred_element_type=F32
    ) + jnp.einsum("efr,efd->erd", up_grad, w_up, preferred_element_type=F32)
    hidden_part = hidden_part.reshape(per_device, groups, shards, CAP, model_width)
    own_part = lax.psum_scatter(hidden_part, "grp", scatter_dimension=1, tiled=True)
    returned = lax.all_to_all(own_part, "shard", split_axis=2, concat_axis=2, tiled=True)
    moe_grad = jnp.einsum(
        "tesc,escd->td",
        token_map.reshape(tokens_here, per_device, shards, CAP),
        returned.reshape(per_device, shards, CAP, model_width),
        precision=lax.Precision.HIGHEST,
        preferred_element_type=F32,
    )
    input_grad = (out_grad.astype(F32) + moe_grad).astype(BF16)
    return (input_grad, grad_gate, grad_up, grad_down)


def solution(mesh):
    groups, shards = mesh.shape["grp"], mesh.shape["shard"]
    per_device = EXPERTS // shards
    tiles = per_device * CAP // TILE
    fits = (
        groups == 4
        and shards & (shards - 1) == 0
        and per_device * CAP == tiles * TILE
        and per_device == PER_TILE * tiles + 1
        and tiles == CAP
    )
    tokens = P(("grp", "shard"), None)
    weights = P("shard", "grp", None)
    return jax.shard_map(
        body if fits else plain_body,
        mesh=mesh,
        in_specs=(tokens, tokens, tokens, tokens, weights, weights, weights),
        out_specs=(tokens, weights, weights, weights),
        check_vma=False,
    )
```

```python
import functools

import jax
import jax.numpy as jnp
from jax import lax
from jax.experimental import pallas as pl
from jax.experimental.pallas import tpu as pltpu
from jax.sharding import PartitionSpec as P

EXPERTS = 128
TOP = 2
CAP = 3
TILE = 16
PER_TILE = TILE // CAP
MESH = pl.DeviceIdType.MESH
F32 = jnp.float32
BF16 = jnp.bfloat16


def silu_parts(pre_act):
    sigmoid_val = jax.nn.sigmoid(pre_act)
    return (pre_act * sigmoid_val, sigmoid_val * (1.0 + pre_act * (1.0 - sigmoid_val)))


def flip(index, bits):
    bit = 1
    while bit <= bits:
        if bits & bit:
            index = index + bit * (1 - 2 * ((index // bit) % 2))
        bit *= 2
    return index


def places(shards):
    grp, me = lax.axis_index("grp"), lax.axis_index("shard")
    peers = [flip(me, k) for k in range(shards)]
    return grp, me, flip(grp, 1), flip(grp, 2), flip(grp, 3), peers


def greet(grp, me, grp_x, grp_y, peers):
    barrier = pltpu.get_barrier_semaphore()
    for peer in peers[1:]:
        pl.semaphore_signal(barrier, inc=1, device_id=(grp, peer), device_id_type=MESH)
    for other in (grp_x, grp_y):
        pl.semaphore_signal(barrier, inc=1, device_id=(other, me), device_id_type=MESH)
    pl.semaphore_wait(barrier, len(peers) + 1)


def remote(src, dst, send_sem, recv_sem, device):
    return pltpu.make_async_remote_copy(
        src_ref=src, dst_ref=dst, send_sem=send_sem, recv_sem=recv_sem,
        device_id=device, device_id_type=MESH,
    )


OWN, BY_X, BY_BOTH, BY_Y = range(4)


def exchange_kernel(order, x_ref, gated_ref, wg_ref, wu_ref, wd_ref, perm_ref, sorted_ref, acts_ref, out_ref,
                    arrived, rows, hidden, parts, weights, from_x, from_y, mid_x, mid_y, end_x, end_y, done,
                    zs, xs, ys, fxs, fys, cx, cy, cx2, cy2, cz, w_sem, own_sem, sorted_sem):
    shards = len(order)
    grp, me, grp_x, grp_y, _, by_flip = places(shards)
    peers = [by_flip[k] for k in order]
    sources = (x_ref, gated_ref)
    kinds, groups, _, depth, width = arrived.shape
    tiles = depth // TILE
    half = shards // 2
    block = groups * half * TILE
    share = groups * half * CAP
    spare = groups * half
    odd = PER_TILE * tiles
    chunk = min(512, width)
    low, high = pl.ds(0, width // 2), pl.ds(width // 2, width // 2)
    by_last = (((1,), (1,)), ((), ()))
    by_first = (((0,), (0,)), ((), ()))
    on_x, on_y = (grp_x, me), (grp_y, me)

    def tile_rows(t):
        return pl.ds(t * TILE, TILE)

    def slots(h):
        return pl.ds(h * half, half)

    def weight_copies(e, slot):
        return [
            pltpu.make_async_copy(ref.at[e], weights.at[j, slot], w_sem.at[j, slot])
            for j, ref in enumerate((wg_ref, wu_ref, wd_ref))
        ]

    def fetch(e, slot):
        for copy in weight_copies(e, slot):
            copy.start()

    def to_neighbours(t, i):
        at = tile_rows(t)
        if i == 0:
            pieces = [(ref.at[me, at], (kind,)) for kind, ref in enumerate(sources)]
        else:
            pieces = [(arrived.at[:, OWN, i, at], (slice(None),))]
        pair = []
        for rel, sems, device in ((BY_X, xs, on_x), (BY_Y, ys, on_y)):
            pair.append([
                remote(src, arrived.at[kind + (rel, i, at)], sems.at[0, t, i, j], sems.at[1, t, i, j], device)
                for j, (src, kind) in enumerate(pieces)
            ])
        for copy in pair[0] + pair[1]:
            copy.start()
        direct[t, i] = pair

    def forward(t, i):
        at = tile_rows(t)
        for copy in direct[t, i][0]:
            copy.wait_recv()
        first = remote(
            arrived.at[0, BY_X, i, at], arrived.at[0, BY_BOTH, i, at], fys.at[0, t, i], fys.at[1, t, i], on_y
        )
        first.start()
        for copy in direct[t, i][1]:
            copy.wait_recv()
        second = remote(
            arrived.at[1, BY_Y, i, at], arrived.at[1, BY_BOTH, i, at], fxs.at[0, t, i], fxs.at[1, t, i], on_x
        )
        second.start()
        passed[t, i] = (first, second)

    def relay(n):
        t, i = steps[n]
        if i > 0:
            for copy in over_z[t, i]:
                copy.wait_recv()
        to_neighbours(t, i)
        if n >= lag:
            forward(*steps[n - lag])

    def sort(t):
        for i in range(shards):
            for copy in passed[t, i]:
                copy.wait_recv()

        def columns(c, _):
            cols = pl.ds(pl.multiple_of(c * chunk, chunk), chunk)
            for kind in range(kinds):
                for side in range(2):
                    part = arrived[
                        kind, :, side * half:(side + 1) * half, t * TILE:(t + 1) * TILE, cols
                    ].reshape(block, chunk)
                    placed = jnp.dot(perm_ref[...], part, preferred_element_type=F32).astype(BF16)
                    for j in range(PER_TILE):
                        rows[kind, t * PER_TILE + j, side * share:(side + 1) * share, cols] = (
                            placed[j * share:(j + 1) * share]
                        )
                    base = (2 * t + side) * spare
                    rows[kind, odd, base:base + spare, cols] = placed[PER_TILE * share:]
            return 0

        lax.fori_loop(0, width // chunk, columns, 0)
        spans = [pl.ds(t * PER_TILE, PER_TILE)] + ([pl.ds(odd, 1)] if t == tiles - 1 else [])
        for j, span in enumerate(spans):
            copy = pltpu.make_async_copy(rows.at[:, span], sorted_ref.at[:, span], sorted_sem.at[t + j])
            copy.start()
            written.append(copy)

    def products(e, slot, span, j):
        for copy in weight_copies(e, slot):
            copy.wait()
        x = rows[0, e, span]
        gated = rows[1, e, span]
        wg, wu = weights[0, slot], weights[1, slot]
        pre_gate = lax.dot_general(x, wg, by_last, preferred_element_type=F32)
        pre_up = lax.dot_general(x, wu, by_last, preferred_element_type=F32)
        act_grad = lax.dot_general(gated, weights[2, slot], by_last, preferred_element_type=F32)
        act_val, act_slope = silu_parts(pre_gate)
        gate_grad = (act_grad * pre_up * act_slope).astype(BF16)
        up_grad = (act_grad * act_val).astype(BF16)
        acts_ref[0, e, span] = (act_val * pre_up).astype(BF16)
        acts_ref[1, e, span] = gate_grad
        acts_ref[2, e, span] = up_grad
        hidden[j, pl.ds(0, span.size)] = (
            jnp.dot(gate_grad, wg, preferred_element_type=F32)
            + jnp.dot(up_grad, wu, preferred_element_type=F32)
        ).astype(BF16)

    def whole_experts(t, begin, end):
        def one(j, _):
            e = t * PER_TILE + j
            fetch(e + 1 + (j + 1) // PER_TILE * (odd - (t + 1) * PER_TILE), (j + 1) % 2)
            products(e, j % 2, pl.ds(0, 2 * share), j)
            return 0

        lax.fori_loop(begin, end, one, 0)

    def odd_expert(t):
        slot = PER_TILE % 2
        if t + 1 < tiles:
            fetch((t + 1) * PER_TILE, 1 - slot)
        products(odd, slot, pl.ds(2 * t * spare, 2 * spare), PER_TILE)

    def unsort(t):
        def columns(c, _):
            cols = pl.ds(pl.multiple_of(c * chunk, chunk), chunk)
            for side in range(2):
                spans = [hidden[j, side * share:(side + 1) * share, cols] for j in range(PER_TILE)]
                spans.append(hidden[PER_TILE, side * spare:(side + 1) * spare, cols])
                back = lax.dot_general(
                    perm_ref[...], jnp.concatenate(spans, axis=0), by_first, preferred_element_type=F32
                ).astype(BF16)
                parts[
                    :, side * half:(side + 1) * half, t * TILE:(t + 1) * TILE, cols
                ] = back.reshape(groups, half, TILE, chunk)
            return 0

        lax.fori_loop(0, width // chunk, columns, 0)

    def first(t, h):
        at = tile_rows(t)
        to_x = remote(
            parts.at[pl.ds(BY_X, 2), slots(h), at, low], from_x.at[t, h], cx.at[0, t, h], cx.at[1, t, h], on_x
        )
        to_y = remote(
            parts.at[pl.ds(BY_BOTH, 2), slots(h), at, high], from_y.at[t, h], cy.at[0, t, h], cy.at[1, t, h], on_y
        )
        to_x.start()
        to_y.start()
        starts[t, h] = (to_x, to_y)

    def second(t, h):
        at = tile_rows(t)
        starts[t, h][0].wait_recv()
        mid_x[t, h] = (parts[BY_Y, slots(h), at, low].astype(F32) + from_x[t, h, 1].astype(F32)).astype(BF16)
        to_y = remote(mid_x.at[t, h], end_y.at[t, h], cy2.at[0, t, h], cy2.at[1, t, h], on_y)
        to_y.start()
        starts[t, h][1].wait_recv()
        mid_y[t, h] = (parts[BY_X, slots(h), at, high].astype(F32) + from_y[t, h, 0].astype(F32)).astype(BF16)
        to_x = remote(mid_y.at[t, h], end_x.at[t, h], cx2.at[0, t, h], cx2.at[1, t, h], on_x)
        to_x.start()
        middles[t, h] = (to_y, to_x)

    def third(t, h):
        at = tile_rows(t)
        middles[t, h][0].wait_recv()
        done[t, h, :, :, low] = (
            parts[OWN, slots(h), at, low].astype(F32) + from_x[t, h, 0].astype(F32) + end_y[t, h].astype(F32)
        ).astype(BF16)
        middles[t, h][1].wait_recv()
        done[t, h, :, :, high] = (
            parts[OWN, slots(h), at, high].astype(F32) + from_y[t, h, 1].astype(F32) + end_x[t, h].astype(F32)
        ).astype(BF16)
        for j in range(half - 1, -1, -1):
            i = h * half + j
            if i == 0:
                out_ref[me, at] = done[t, h, 0]
            else:
                copy = remote(
                    done.at[t, h, j], out_ref.at[me, at], cz.at[0, t, i], cz.at[1, t, i], (grp, peers[i])
                )
                copy.start()
                returns.append(copy)

    direct, over_z, passed, starts, middles = {}, {}, {}, {}, {}
    returns, written = [], []
    steps = [(t, i) for t in range(tiles) for i in range(shards)]
    lag = 3
    fetch(0, 0)
    greet(grp, me, grp_x, grp_y, by_flip)
    relay(0)
    for t, i in steps:
        if i > 0:
            over_z[t, i] = [
                remote(
                    ref.at[peers[i], tile_rows(t)], arrived.at[kind, OWN, i, tile_rows(t)],
                    zs.at[0, t, i, kind], zs.at[1, t, i, kind], (grp, peers[i]),
                )
                for kind, ref in enumerate(sources)
            ]
            for copy in over_z[t, i]:
                copy.start()
    own = [
        pltpu.make_async_copy(ref.at[me], arrived.at[kind, OWN, 0], own_sem.at[kind])
        for kind, ref in enumerate(sources)
    ]
    for copy in own:
        copy.start()

    def work(t):
        tasks = [functools.partial(sort, t)]
        tasks += [functools.partial(whole_experts, t, j, j + 1) for j in range(PER_TILE)]
        return tasks + [functools.partial(odd_expert, t), functools.partial(unsort, t)]

    queue = []
    for n in range(1, len(steps)):
        relay(n)
        t, i = steps[n]
        if t == 0:
            continue
        if i == lag + 1:
            if t == 1:
                for copy in own:
                    copy.wait()
            queue += work(t - 1)
        for task in queue[:2]:
            task()
        queue = queue[2:]
        if t == 2 and i == 2:
            first(0, 0)
        if t == 2 and i == lag + 2:
            first(0, 1)
    for task in queue:
        task()
    for n in range(len(steps) - lag, len(steps)):
        forward(*steps[n])
    for t in range(1, tiles - 1):
        first(t, 0)
        first(t, 1)
    second(0, 0)
    tasks = work(tiles - 1)
    tasks[0]()
    units = [(t, h) for t in range(tiles - 1) for h in range(2)]
    for j, task in enumerate(tasks[1:]):
        task()
        if j + 1 < len(units):
            second(*units[j + 1])
        if j < len(units):
            third(*units[j])
    first(tiles - 1, 0)
    first(tiles - 1, 1)
    second(tiles - 1, 0)
    second(tiles - 1, 1)
    third(tiles - 1, 0)
    third(tiles - 1, 1)
    for step in steps:
        if step[1] > 0:
            for copy in over_z[step]:
                copy.wait_send()
        for copy in direct[step][0] + direct[step][1] + list(passed[step]):
            copy.wait_send()
    for unit in starts:
        for copy in starts[unit] + middles[unit]:
            copy.wait_send()
    for copy in written:
        copy.wait()
    for copy in returns:
        copy.wait()


def sort_matrix(sources):
    taken = jnp.arange(sources * TILE, dtype=jnp.int32)
    source, place = taken // TILE, taken % TILE
    goes = jnp.where(
        place < PER_TILE * CAP,
        place // CAP * (sources * CAP) + source * CAP + place % CAP,
        PER_TILE * CAP * sources + source,
    )
    return (goes[None, :] == taken[:, None]).astype(BF16)


def exchange(sent, gated, w_gate, w_up, w_down, groups):
    shards, depth, width = sent.shape
    count, units, _ = w_gate.shape
    row_count = groups * shards * CAP
    tiles = depth // TILE
    order = sorted(range(shards), key=lambda k: (k // 2 % 2, k))
    perm = sort_matrix(groups * shards // 2)
    half = pltpu.VMEM((tiles, 2, shards // 2, TILE, width // 2), BF16)
    pair = pltpu.VMEM((tiles, 2, 2, shards // 2, TILE, width // 2), BF16)
    sem = pltpu.SemaphoreType.DMA((2, tiles, shards))
    sem_kinds = pltpu.SemaphoreType.DMA((2, tiles, shards, 2))
    sem_halves = pltpu.SemaphoreType.DMA((2, tiles, 2))
    anywhere = pl.BlockSpec(memory_space=pl.ANY)
    near = pl.BlockSpec(memory_space=pltpu.VMEM)
    return pl.pallas_call(
        functools.partial(exchange_kernel, order),
        out_shape=(
            jax.ShapeDtypeStruct((2, count, row_count, width), BF16),
            jax.ShapeDtypeStruct((3, count, row_count, units), BF16),
            jax.ShapeDtypeStruct((shards, depth, width), BF16),
        ),
        in_specs=[anywhere] * 5 + [near],
        out_specs=(anywhere, near, near),
        scratch_shapes=[
            pltpu.VMEM((2, groups, shards, depth, width), BF16),
            pltpu.VMEM((2, count, row_count, width), BF16),
            pltpu.VMEM((PER_TILE + 1, row_count, width), BF16),
            pltpu.VMEM((groups, shards, depth, width), BF16),
            pltpu.VMEM((3, 2, units, width), BF16),
            pair, pair, half, half, half, half,
            pltpu.VMEM((tiles, 2, shards // 2, TILE, width), BF16),
            sem_kinds, sem_kinds, sem_kinds, sem, sem,
            sem_halves, sem_halves, sem_halves, sem_halves, sem,
            pltpu.SemaphoreType.DMA((3, 2)),
            pltpu.SemaphoreType.DMA((2,)),
            pltpu.SemaphoreType.DMA((tiles + 1,)),
        ],
        compiler_params=pltpu.CompilerParams(
            collective_id=0, has_side_effects=True, vmem_limit_bytes=60 * 1024 * 1024
        ),
        name="exchange",
    )(sent, gated, w_gate, w_up, w_down, perm)


def grads_kernel(rows_ref, acts_ref, gg_ref, gu_ref, gd_ref):
    by_first = (((0,), (0,)), ((), ()))
    x, gated = rows_ref[0, 0], rows_ref[1, 0]
    for ref, j, side in ((gd_ref, 0, gated), (gg_ref, 1, x), (gu_ref, 2, x)):
        ref[0] = lax.dot_general(acts_ref[j, 0], side, by_first, preferred_element_type=F32).astype(BF16)


def grads(rows, acts):
    kinds, count, row_count, width = rows.shape
    units = acts.shape[-1]
    grad = jax.ShapeDtypeStruct((count, units, width), BF16)
    out = pl.BlockSpec((1, units, width), lambda e: (e, 0, 0))
    return pl.pallas_call(
        grads_kernel,
        grid=(count,),
        out_shape=(grad, grad, grad),
        in_specs=[
            pl.BlockSpec((kinds, 1, row_count, width), lambda e: (0, e, 0, 0)),
            pl.BlockSpec((3, 1, row_count, units), lambda e: (0, e, 0, 0)),
        ],
        out_specs=(out, out, out),
        compiler_params=pltpu.CompilerParams(vmem_limit_bytes=60 * 1024 * 1024),
        name="grads",
    )(rows, acts)


def body(moe_input, out_grad, expert_ids, gate_weights, w_gate, w_up, w_down):
    contract_rows = (((0,), (0,)), ((), ()))
    shards = lax.axis_size("shard")
    groups = lax.axis_size("grp")
    per_device = w_gate.shape[0]
    tokens_here, model_width = moe_input.shape
    depth = per_device * CAP
    tiles = depth // TILE
    flat_ids = expert_ids.reshape(tokens_here * TOP)
    matches = (flat_ids[:, None] == jnp.arange(EXPERTS, dtype=jnp.int32)[None, :]).astype(jnp.int32)
    rank_of = jnp.sum((jnp.cumsum(matches, axis=0) - matches) * matches, axis=1)
    local = flat_ids % per_device
    odd = PER_TILE * tiles
    place = jnp.where(
        local < odd,
        local // PER_TILE * TILE + local % PER_TILE * CAP + rank_of,
        rank_of * TILE + PER_TILE * CAP,
    )
    slot_of = (flat_ids // per_device * depth + place).reshape(tokens_here, TOP)
    slots = jnp.arange(EXPERTS * CAP, dtype=jnp.int32)
    chosen = slot_of[:, :, None] == slots[None, None, :]
    token_map = jnp.any(chosen, axis=1).astype(BF16)
    gate_map = jnp.sum(
        jnp.where(chosen, gate_weights.astype(F32)[:, :, None], 0.0), axis=1
    ).astype(BF16)
    input_slots = lax.dot_general(token_map, moe_input, contract_rows, preferred_element_type=F32)
    gated_slots = lax.dot_general(gate_map, out_grad, contract_rows, preferred_element_type=F32)
    block = (shards, depth, model_width)
    sorted_rows, acts, returned = exchange(
        input_slots.astype(BF16).reshape(block), gated_slots.astype(BF16).reshape(block),
        w_gate, w_up, w_down, groups,
    )
    grad_gate, grad_up, grad_down = grads(sorted_rows, acts)
    returned = returned.reshape(shards * depth, model_width)
    moe_grad = jnp.dot(token_map, returned, preferred_element_type=F32)
    input_grad = (out_grad.astype(F32) + moe_grad).astype(BF16)
    return (input_grad, grad_gate, grad_up, grad_down)


def plain_slot_maps(ids_here, per_device, shards):
    tokens_here = ids_here.shape[0]
    flat_ids = ids_here.reshape(tokens_here * TOP)
    matches = (flat_ids[:, None] == jnp.arange(EXPERTS, dtype=jnp.int32)[None, :]).astype(jnp.int32)
    rank_of = jnp.sum((jnp.cumsum(matches, axis=0) - matches) * matches, axis=1)
    slot_of = flat_ids % per_device * (shards * CAP) + flat_ids // per_device * CAP + rank_of
    return (slot_of[:, None] == jnp.arange(EXPERTS * CAP, dtype=jnp.int32)[None, :]).astype(F32)


def plain_body(moe_input, out_grad, expert_ids, gate_weights, w_gate, w_up, w_down):
    contract_rows = (((0,), (0,)), ((), ()))
    shards = lax.axis_size("shard")
    groups = lax.axis_size("grp")
    per_device = w_gate.shape[0]
    tokens_here, model_width = moe_input.shape
    slot_total = EXPERTS * CAP
    chosen = plain_slot_maps(expert_ids, per_device, shards).reshape(tokens_here, TOP, slot_total)
    token_map = jnp.sum(chosen, axis=1)
    gate_map = jnp.sum(chosen * gate_weights.astype(F32)[:, :, None], axis=1).astype(BF16)
    slot_shape = (per_device, shards, CAP, model_width)
    row_count = groups * shards * CAP

    def send(mapping, rows):
        slots = lax.dot_general(mapping, rows, contract_rows, preferred_element_type=F32).astype(BF16)
        arrived = lax.all_to_all(
            slots.reshape(slot_shape), "shard", split_axis=1, concat_axis=1, tiled=True
        )
        gathered = lax.all_gather(arrived, "grp", axis=1, tiled=True)
        return gathered.reshape(per_device, row_count, model_width)

    inputs = send(token_map.astype(BF16), moe_input)
    gated = send(gate_map, out_grad)
    pre_gate = jnp.einsum("efd,erd->efr", w_gate, inputs, preferred_element_type=F32)
    pre_up = jnp.einsum("efd,erd->efr", w_up, inputs, preferred_element_type=F32)
    act_val, act_slope = silu_parts(pre_gate)
    activation = (act_val * pre_up).astype(BF16)
    act_grad = jnp.einsum("efd,erd->efr", w_down, gated, preferred_element_type=F32)
    gate_grad = (act_grad * pre_up * act_slope).astype(BF16)
    up_grad = (act_grad * act_val).astype(BF16)
    grad_down = jnp.einsum("efr,erd->efd", activation, gated, preferred_element_type=F32).astype(BF16)
    grad_gate = jnp.einsum("efr,erd->efd", gate_grad, inputs, preferred_element_type=F32).astype(BF16)
    grad_up = jnp.einsum("efr,erd->efd", up_grad, inputs, preferred_element_type=F32).astype(BF16)
    hidden_part = jnp.einsum(
        "efr,efd->erd", gate_grad, w_gate, preferred_element_type=F32
    ) + jnp.einsum("efr,efd->erd", up_grad, w_up, preferred_element_type=F32)
    hidden_part = hidden_part.reshape(per_device, groups, shards, CAP, model_width)
    own_part = lax.psum_scatter(hidden_part, "grp", scatter_dimension=1, tiled=True)
    returned = lax.all_to_all(own_part, "shard", split_axis=2, concat_axis=2, tiled=True)
    moe_grad = jnp.einsum(
        "tesc,escd->td",
        token_map.reshape(tokens_here, per_device, shards, CAP),
        returned.reshape(per_device, shards, CAP, model_width),
        precision=lax.Precision.HIGHEST,
        preferred_element_type=F32,
    )
    input_grad = (out_grad.astype(F32) + moe_grad).astype(BF16)
    return (input_grad, grad_gate, grad_up, grad_down)


def solution(mesh):
    groups, shards = mesh.shape["grp"], mesh.shape["shard"]
    per_device = EXPERTS // shards
    tiles = per_device * CAP // TILE
    fits = (
        groups == 4
        and shards & (shards - 1) == 0
        and per_device * CAP == tiles * TILE
        and per_device == PER_TILE * tiles + 1
        and tiles == CAP
    )
    tokens = P(("grp", "shard"), None)
    weights = P("shard", "grp", None)
    return jax.shard_map(
        body if fits else plain_body,
        mesh=mesh,
        in_specs=(tokens, tokens, tokens, tokens, weights, weights, weights),
        out_specs=(tokens, weights, weights, weights),
        check_vma=False,
    )
```
